32 devices in a mesh: tile: 8 (over z, core), view: 4 (over y, x).
Axes of the slice: x: 2, y: 2, z: 4, core: 2. Of those that a mesh axis runs over, the one named last changes fastest.
Arguments:
- estimate: float32 [128, 128, 256], P('tile', 'view'), may hold values from 0.5 to 2
- observed: float32 [4, 8, 26, 128, 256], P('view', 'tile'), may hold values from 0.25 to 4
- psf: float32 [12, 3, 11], replicated, may hold values from 0.1 to 1
- cover: int32 [8, 4], replicated, may hold values from 0 to 12, as said below
- offsets: int32 [8, 4], replicated, may hold values from -5 to 5
Outputs:
- updated: float32 [128, 128, 256], P('tile', 'view')
The draws below stay inside these ranges and needn't reach their ends.
Inputs may be any that keep to these rules, and one draw needn't show every extreme that they name: `cover`: slot 0 of every block holds a view; slot 1 of block 0 is empty; other slots are empty with probability 0.4.
All inputs are finite; a program needn't handle non-finite values.
Results may differ from the reference program's by a relative error of at most 0.0003.
Values sent between devices are 32-bit elements; how exact they have to be, the bound alone decides.
A program may use at most 64 MiB of HBM per device.

```python
import math
import jax
import jax.numpy as jnp
from jax import lax

TX = 16
NY = 128
NZ = 256
K = 11
VIEWS = 12
ITERS = 2
RADIUS = 5
TILES = 8
SLOTS = 4
NX = 128


def draw_cover(key, part):
    key_views, key_empty = jax.random.split(key)
    view_ids = jax.random.randint(key_views, (TILES, SLOTS), 0, VIEWS)
    is_empty = jax.random.randint(key_empty, (TILES, SLOTS), 0, 5) < 2
    slot_ids = jnp.arange(SLOTS)[None, :]
    tile_ids = jnp.arange(TILES)[:, None]
    is_empty = jnp.where(slot_ids == 0, False, is_empty)
    is_empty = jnp.where((tile_ids == 0) & (slot_ids == 1), True, is_empty)
    return jnp.where(is_empty, VIEWS, view_ids).astype(jnp.int32)


def plant(array, rng, low, high):
    longest = array.shape.index(max(array.shape))
    spots = []
    for shift in (0, 1):
        where = [jax.random.randint(jax.random.fold_in(rng, axis), (), 0, length) for axis, length in enumerate(array.shape)]
        where[longest] = (where[longest] + shift) % array.shape[longest]
        spots.append(tuple(where))
    return array.at[spots[0]].set(low).at[spots[1]].set(high)


def shard_levels(key, dims, shards, smallest, top_value):
    gain, own = 1.0, jax.random.fold_in(key, 6)
    for dim, parts in shards:
        draws = jnp.exp(jax.random.uniform(jax.random.fold_in(own, dim), (parts,), jnp.float32, smallest / len(shards), top_value / len(shards)))
        gain = gain * jnp.repeat(draws, dims[dim] // parts).reshape([-1 if axis == dim else 1 for axis in range(len(dims))])
    return gain


def setup_inputs(seed: int = 0) -> dict:
    arg_keys = jax.random.split(jax.random.key(seed), 6)
    estimate = jnp.clip(jnp.exp(math.log(2.0) - 1.3862944 * jax.random.uniform(arg_keys[0], (NX, NY, NZ), jnp.float32) ** shard_levels(arg_keys[0], (NX, NY, NZ), ((0, 8), (1, 4)), -0.2, 0.2)), 0.5, 2.0)
    observed = jnp.clip(jnp.exp(math.log(4.0) - 2.7725887 * jax.random.uniform(arg_keys[1], (SLOTS, TILES, TX + 2 * RADIUS, NY, NZ), jnp.float32) ** shard_levels(arg_keys[1], (SLOTS, TILES, TX + 2 * RADIUS, NY, NZ), ((0, 4), (1, 8)), -0.2, 0.2)), 0.25, 4.0)
    psf = jnp.clip(jnp.exp(jax.random.uniform(arg_keys[2], (VIEWS, 3, K), jnp.float32, math.log(0.1), math.log(1.0))), 0.1, 1.0)
    cover = draw_cover(jax.random.fold_in(arg_keys[5], 71), 0)
    offsets = plant(jax.random.randint(arg_keys[4], (TILES, SLOTS), 0 - RADIUS, RADIUS + 1), jax.random.fold_in(arg_keys[4], 1), 0 - RADIUS, RADIUS).astype(jnp.int32)
    return {"estimate": estimate, "observed": observed, "psf": psf, "cover": cover, "offsets": offsets}


def band_matrix(taps, rows, cols, z_offset, limit):
    radius = taps.shape[0] // 2
    offset = cols[None, :] - rows[:, None] - z_offset + radius
    inside = (cols[None, :] >= 0) & (cols[None, :] < limit)
    tap_index = jnp.arange(taps.shape[0], dtype=jnp.int32)
    weight = jnp.sum(jnp.where(offset[:, :, None] == tap_index, taps, 0.0), axis=2)
    weight = jnp.where(inside, weight, 0.0)
    return weight / jnp.sum(weight, axis=1, keepdims=True)


def view_kernels(psf, view_id):
    clipped = jnp.minimum(view_id, psf.shape[0] - 1)
    select = (jnp.arange(psf.shape[0], dtype=jnp.int32) == clipped).astype(psf.dtype)
    return jnp.sum(psf * select[:, None, None], axis=0)


def slot_back(extended, view_data, kernels, z_offset, first_row, total_rows, tile_rows):
    radius = kernels.shape[1] // 2
    exact = lax.Precision.HIGHEST
    rows = first_row - radius + jnp.arange(tile_rows + 2 * radius, dtype=jnp.int32)
    cols = first_row - 2 * radius + jnp.arange(tile_rows + 4 * radius, dtype=jnp.int32)
    x_weights = band_matrix(kernels[0], rows, cols, 0, total_rows)
    y_cells = jnp.arange(extended.shape[1], dtype=jnp.int32)
    z_cells = jnp.arange(extended.shape[2], dtype=jnp.int32)
    y_weights = band_matrix(kernels[1], y_cells, y_cells, 0, extended.shape[1])
    z_weights = band_matrix(kernels[2], z_cells, z_cells, z_offset, extended.shape[2])
    blurred = jnp.einsum('ij,jyz->iyz', x_weights, extended, precision=exact)
    blurred = jnp.einsum('yw,iwz->iyz', y_weights, blurred, precision=exact)
    blurred = jnp.einsum('iyw,zw->iyz', blurred, z_weights, precision=exact)
    in_range = ((rows >= 0) & (rows < total_rows)).astype(blurred.dtype)
    quotient = in_range[:, None, None] * view_data / blurred
    interior = x_weights[:, 2 * radius:2 * radius + tile_rows]
    back_blur = jnp.einsum('ri,ryz->iyz', interior, quotient, precision=exact)
    back_blur = jnp.einsum('wy,iwz->iyz', y_weights, back_blur, precision=exact)
    back_blur = jnp.einsum('iyw,wz->iyz', back_blur, z_weights, precision=exact)
    return back_blur


def reference(estimate, observed, psf, cover, offsets):
    for sweep_index in range(ITERS):
        padded = jnp.pad(estimate, ((2 * RADIUS, 2 * RADIUS), (0, 0), (0, 0)))

        def tile_update(tile_index):
            first_row = tile_index * TX
            extended = lax.dynamic_slice_in_dim(padded, first_row, TX + 4 * RADIUS, 0)
            current = lax.dynamic_slice_in_dim(estimate, first_row, TX, 0)

            def one_slot(slot_index):
                view_id = cover[tile_index, slot_index]
                kernels = view_kernels(psf, view_id)
                view_data = observed[slot_index, tile_index]
                result = slot_back(extended, view_data, kernels, offsets[tile_index, slot_index], first_row, NX, TX)
                return jnp.where(view_id < VIEWS, result, 0.0)

            summed = jnp.sum(lax.map(one_slot, jnp.arange(SLOTS, dtype=jnp.int32)), axis=0)
            coverage = jnp.sum((cover[tile_index] < VIEWS).astype(jnp.float32))
            return current * summed / coverage

        estimate = lax.map(tile_update, jnp.arange(TILES, dtype=jnp.int32)).reshape(NX, NY, NZ)
    return estimate
```

```python
import functools

import jax
import jax.numpy as jnp
from jax import lax
from jax.experimental import pallas as pl
from jax.experimental.pallas import tpu as pltpu
from jax.sharding import PartitionSpec as P

ITERS = 2


def split(x):
    high = x.astype(jnp.bfloat16)
    low = (x - high.astype(jnp.float32)).astype(jnp.bfloat16)
    return high, low


def dot(a, b):
    return jnp.dot(a, b, preferred_element_type=jnp.float32)


def dot3(a, b):
    (ah, al), (bh, bl) = a, b
    return dot(ah, bh) + (dot(ah, bl) + dot(al, bh))


def kernel(
    tiles, slots, est, obs_hbm, psf, cover, offsets, out,
    cells, mid, obs, sent, got, own, wz, wzt, wy, wyt,
    obs_sem, gs, gr, hs, hr, rs, rr,
):
    t = lax.axis_index("tile")
    s = lax.axis_index("view")
    rows, share, nz = est.shape
    ny = mid.shape[1]
    views, _, taps = psf.shape
    rad = taps // 2
    wide = rows + 2 * rad
    has_prev, has_next = t > 0, t < tiles - 1

    def cols(d):
        return pl.ds(pl.multiple_of(lax.rem(s + slots - d, slots) * share, 8), share)

    def peer(d):
        return {"view": lax.rem(s + d, slots)}

    obs_copy = pltpu.make_async_copy(obs_hbm.at[0, 0], obs, obs_sem)
    obs_copy.start()

    barrier = pltpu.get_barrier_semaphore()
    for d in range(1, slots):
        pl.semaphore_signal(barrier, inc=1, device_id=peer(d), device_id_type=pl.DeviceIdType.MESH)

    @pl.when(has_prev)
    def _():
        pl.semaphore_signal(barrier, inc=1, device_id={"tile": t - 1}, device_id_type=pl.DeviceIdType.MESH)

    @pl.when(has_next)
    def _():
        pl.semaphore_signal(barrier, inc=1, device_id={"tile": t + 1}, device_id_type=pl.DeviceIdType.MESH)

    neighbours = has_prev.astype(jnp.int32) + has_next.astype(jnp.int32)
    pl.semaphore_wait(barrier, slots - 1 + neighbours)

    def gather(b, d):
        src = est if b == 0 else cells.at[b, pl.ds(2 * rad, rows), cols(0), :]
        return pltpu.make_async_remote_copy(
            src_ref=src,
            dst_ref=cells.at[b, pl.ds(2 * rad, rows), cols(0), :],
            send_sem=gs.at[b, d], recv_sem=gr.at[b, d],
            device_id=peer(d), device_id_type=pl.DeviceIdType.MESH,
        )

    def gather_in(b, d):
        block = cells.at[b, pl.ds(2 * rad, rows), cols(d), :]
        return pltpu.make_async_remote_copy(
            src_ref=block, dst_ref=block,
            send_sem=gs.at[b, d], recv_sem=gr.at[b, d],
            device_id=peer(d), device_id_type=pl.DeviceIdType.MESH,
        )

    def halo(b, d, up):
        first, to = (rows, 0) if up else (2 * rad, rows + 2 * rad)
        return pltpu.make_async_remote_copy(
            src_ref=cells.at[b, pl.ds(first, 2 * rad), cols(d), :],
            dst_ref=cells.at[b, pl.ds(to, 2 * rad), cols(d), :],
            send_sem=hs.at[b, d, int(up)], recv_sem=hr.at[b, d, int(up)],
            device_id={"tile": t + 1 if up else t - 1}, device_id_type=pl.DeviceIdType.MESH,
        )

    def halo_start(b, d):
        @pl.when(has_next)
        def _():
            halo(b, d, True).start()

        @pl.when(has_prev)
        def _():
            halo(b, d, False).start()

    def halo_wait(b, d):
        @pl.when(has_prev)
        def _():
            halo(b, d, True).wait_recv()

        @pl.when(has_next)
        def _():
            halo(b, d, False).wait_recv()

    def halo_sent(b, d):
        @pl.when(has_next)
        def _():
            halo(b, d, True).wait_send()

        @pl.when(has_prev)
        def _():
            halo(b, d, False).wait_send()

    def scatter(b, d):
        return pltpu.make_async_remote_copy(
            src_ref=sent.at[b, d - 1], dst_ref=got.at[b, d - 1],
            send_sem=rs.at[b, d], recv_sem=rr.at[b, d],
            device_id=peer(d), device_id_type=pl.DeviceIdType.MESH,
        )

    view = cover[t, s]
    clipped = jnp.minimum(view, views - 1)
    shift = offsets[t, s]
    count = jnp.float32(0.0)
    for d in range(slots):
        count = count + jnp.where(cover[t, d] < views, 1.0, 0.0)
    scale = jnp.where(view < views, 1.0, 0.0) / jnp.full((8, nz), count, jnp.float32)
    bx = [psf[clipped, 0, k] for k in range(taps)]

    def band(size, axis, offset, high, low, transposed):
        r = lax.broadcasted_iota(jnp.int32, (size, size), 1 if transposed else 0)
        c = lax.broadcasted_iota(jnp.int32, (size, size), 0 if transposed else 1)
        where = c - r - offset + rad
        weight = jnp.zeros((size, size), jnp.float32)
        for k in range(taps):
            weight = jnp.where(where == k, psf[clipped, axis, k], weight)
        h, l = split(weight)
        high[...] = h
        low[...] = l

    def forward(b, d):
        base = lax.rem(s + slots - d, slots) * share

        @pl.loop(0, share // 8)
        def _(i):
            at = pl.ds(pl.multiple_of(base + i * 8, 8), 8)
            x = [cells[b, j, at, :] for j in range(rows + 4 * rad)]
            sums = []
            for r in range(wide):
                total = bx[0] * x[r]
                for k in range(1, taps):
                    total = total + bx[k] * x[r + k]
                sums.append(total)
            data = split(jnp.concatenate(sums, axis=0))
            z = dot3(data, (wzt[0], wzt[1]))
            mid[:, at, :] = z.reshape(wide, 8, nz)

    def middle():
        @pl.loop(0, wide)
        def _(r):
            row = t * rows - rad + r
            inside = jnp.logical_and(row >= 0, row < tiles * rows)
            blurred = dot3((wy[0], wy[1]), split(mid[r]))
            quotient = jnp.where(inside, obs[r], 0.0) / blurred
            mid[r] = dot3((wyt[0], wyt[1]), split(quotient))

    def backward(d, put):
        base = lax.rem(s + d, slots) * share

        @pl.loop(0, share // 8)
        def _(i):
            at = pl.ds(pl.multiple_of(base + i * 8, 8), 8)
            q = [mid[j, at, :] for j in range(wide)]
            sums = []
            for r in range(rows):
                total = bx[0] * q[r + 2 * rad]
                for k in range(1, taps):
                    total = total + bx[k] * q[r + 2 * rad - k]
                sums.append(total)
            data = split(jnp.concatenate(sums, axis=0))
            z = dot3(data, (wz[0], wz[1])).reshape(rows, 8, nz) * scale[None]
            put(pl.ds(pl.multiple_of(i * 8, 8), 8), z)

    for b in range(ITERS):
        for d in range(1, slots):
            gather(b, d).start()
        if b == 0:
            cells[0, pl.ds(2 * rad, rows), cols(0), :] = est[...]
        halo_start(b, 0)

        @pl.when(jnp.logical_not(has_prev))
        def _():
            cells[b, pl.ds(0, 2 * rad), :, :] = jnp.zeros((2 * rad, ny, nz), jnp.float32)

        @pl.when(jnp.logical_not(has_next))
        def _():
            cells[b, pl.ds(rows + 2 * rad, 2 * rad), :, :] = jnp.zeros((2 * rad, ny, nz), jnp.float32)

        if b == 0:
            band(nz, 2, shift, wzt.at[0], wzt.at[1], True)
            band(nz, 2, shift, wz.at[0], wz.at[1], False)
            band(ny, 1, 0, wy.at[0], wy.at[1], False)
            band(ny, 1, 0, wyt.at[0], wyt.at[1], True)
        for d in range(1, slots + 1):
            if d < slots:
                gather_in(b, d).wait_recv()
                halo_start(b, d)
            halo_wait(b, d - 1)
            forward(b, d - 1)
        if b == 0:
            obs_copy.wait()
        middle()
        for d in range(1, slots):
            def put(at, z, d=d):
                sent[b, d - 1, :, at, :] = z

            backward(d, put)
            scatter(b, d).start()

        def keep(at, z):
            own[:, at, :] = z

        backward(0, keep)
        for d in range(1, slots):
            scatter(b, d).wait_recv()
        target = out if b == ITERS - 1 else None

        @pl.loop(0, rows)
        def _(r):
            total = own[r]
            for d in range(1, slots):
                total = total + got[b, d - 1, r]
            new = cells[b, 2 * rad + r, cols(0), :] * total
            if target is not None:
                out[r] = new
            else:
                cells[b + 1, 2 * rad + r, cols(0), :] = new

    for b in range(ITERS):
        for d in range(slots):
            if d:
                gather(b, d).wait_send()
                scatter(b, d).wait_send()
            halo_sent(b, d)


def per_device(tiles, slots, estimate, observed, psf, cover, offsets):
    rows, share, nz = estimate.shape
    wide, ny = observed.shape[2:4]
    f32, bf16, dma = jnp.float32, jnp.bfloat16, pltpu.SemaphoreType.DMA
    vmem = pl.BlockSpec(memory_space=pltpu.VMEM)
    smem = pl.BlockSpec(memory_space=pltpu.SMEM)
    return pl.pallas_call(
        functools.partial(kernel, tiles, slots),
        out_shape=jax.ShapeDtypeStruct(estimate.shape, f32),
        in_specs=[vmem, pl.BlockSpec(memory_space=pl.ANY), smem, smem, smem],
        out_specs=vmem,
        scratch_shapes=[
            pltpu.VMEM((ITERS, 2 * wide - rows, ny, nz), f32),
            pltpu.VMEM((wide, ny, nz), f32),
            pltpu.VMEM((wide, ny, nz), f32),
            pltpu.VMEM((ITERS, slots - 1, rows, share, nz), f32),
            pltpu.VMEM((ITERS, slots - 1, rows, share, nz), f32),
            pltpu.VMEM((rows, share, nz), f32),
            pltpu.VMEM((2, nz, nz), bf16),
            pltpu.VMEM((2, nz, nz), bf16),
            pltpu.VMEM((2, ny, ny), bf16),
            pltpu.VMEM((2, ny, ny), bf16),
            dma,
            dma((ITERS, slots)), dma((ITERS, slots)),
            dma((ITERS, slots, 2)), dma((ITERS, slots, 2)),
            dma((ITERS, slots)), dma((ITERS, slots)),
        ],
        compiler_params=pltpu.CompilerParams(
            collective_id=0, has_side_effects=True, vmem_limit_bytes=48 * 1024 * 1024
        ),
    )(estimate, observed, psf, cover, offsets)


def solution(mesh):
    placed = (P("tile", "view", None), P("view", "tile", None, None, None), P(), P(), P())
    return jax.shard_map(
        functools.partial(per_device, mesh.shape["tile"], mesh.shape["view"]),
        mesh=mesh, in_specs=placed, out_specs=P("tile", "view", None), check_vma=False,
    )
```

```python
import functools

import jax
import jax.numpy as jnp
from jax import lax
from jax.experimental import pallas as pl
from jax.experimental.pallas import tpu as pltpu
from jax.sharding import PartitionSpec as P

ITERS = 2


def split(x):
    high = x.astype(jnp.bfloat16)
    low = (x - high.astype(jnp.float32)).astype(jnp.bfloat16)
    return high, low


def dot(a, b):
    return jnp.dot(a, b, preferred_element_type=jnp.float32)


def dot3(a, b):
    (ah, al), (bh, bl) = a, b
    return dot(ah, bh) + (dot(ah, bl) + dot(al, bh))


def kernel(
    tiles, slots, est, obs_hbm, psf, cover, offsets, out,
    cells, mid, obs, sent, got, own, wz, wzt, wy, wyt,
    obs_sem, gs, gr, hs, hr, rs, rr,
):
    t = lax.axis_index("tile")
    s = lax.axis_index("view")
    rows, share, nz = est.shape
    ny = mid.shape[1]
    views, _, taps = psf.shape
    rad = taps // 2
    wide = rows + 2 * rad
    has_prev, has_next = t > 0, t < tiles - 1

    half = rows // 2
    grid = slots == 4
    around = (s, s + 1 - 2 * lax.rem(s, 2), lax.rem(s + 2, 4), 3 - s)

    def source(d):
        return around[d] if grid else lax.rem(s + slots - d, slots)

    def goal(d):
        return around[d] if grid else lax.rem(s + d, slots)

    def cols(d):
        return pl.ds(pl.multiple_of(source(d) * share, 8), share)

    def peer(d):
        return {"view": goal(d)}

    obs_copy = pltpu.make_async_copy(obs_hbm.at[0, 0], obs, obs_sem)
    obs_copy.start()

    barrier = pltpu.get_barrier_semaphore()
    for d in range(1, slots):
        pl.semaphore_signal(barrier, inc=1, device_id=peer(d), device_id_type=pl.DeviceIdType.MESH)

    @pl.when(has_prev)
    def _():
        pl.semaphore_signal(barrier, inc=1, device_id={"tile": t - 1}, device_id_type=pl.DeviceIdType.MESH)

    @pl.when(has_next)
    def _():
        pl.semaphore_signal(barrier, inc=1, device_id={"tile": t + 1}, device_id_type=pl.DeviceIdType.MESH)

    neighbours = has_prev.astype(jnp.int32) + has_next.astype(jnp.int32)
    pl.semaphore_wait(barrier, slots - 1 + neighbours)

    def gather(b, d):
        src = est if b == 0 else cells.at[b, pl.ds(2 * rad, rows), cols(0), :]
        return pltpu.make_async_remote_copy(
            src_ref=src,
            dst_ref=cells.at[b, pl.ds(2 * rad, rows), cols(0), :],
            send_sem=gs.at[b, d], recv_sem=gr.at[b, d],
            device_id=peer(d), device_id_type=pl.DeviceIdType.MESH,
        )

    def gather_in(b, d):
        block = cells.at[b, pl.ds(2 * rad, rows), cols(d), :]
        return pltpu.make_async_remote_copy(
            src_ref=block, dst_ref=block,
            send_sem=gs.at[b, d], recv_sem=gr.at[b, d],
            device_id=peer(d), device_id_type=pl.DeviceIdType.MESH,
        )

    def halo(b, d, up):
        first, to = (rows, 0) if up else (2 * rad, rows + 2 * rad)
        return pltpu.make_async_remote_copy(
            src_ref=cells.at[b, pl.ds(first, 2 * rad), cols(d), :],
            dst_ref=cells.at[b, pl.ds(to, 2 * rad), cols(d), :],
            send_sem=hs.at[b, d, int(up)], recv_sem=hr.at[b, d, int(up)],
            device_id={"tile": t + 1 if up else t - 1}, device_id_type=pl.DeviceIdType.MESH,
        )

    def halo_start(b, d):
        @pl.when(has_next)
        def _():
            halo(b, d, True).start()

        @pl.when(has_prev)
        def _():
            halo(b, d, False).start()

    def halo_wait(b, d):
        @pl.when(has_prev)
        def _():
            halo(b, d, True).wait_recv()

        @pl.when(has_next)
        def _():
            halo(b, d, False).wait_recv()

    def halo_sent(b, d):
        @pl.when(has_next)
        def _():
            halo(b, d, True).wait_send()

        @pl.when(has_prev)
        def _():
            halo(b, d, False).wait_send()

    def scatter(b, d):
        return pltpu.make_async_remote_copy(
            src_ref=sent.at[b, d - 1], dst_ref=got.at[b, d - 1],
            send_sem=rs.at[b, d], recv_sem=rr.at[b, d],
            device_id=peer(d), device_id_type=pl.DeviceIdType.MESH,
        )

    view = cover[t, s]
    clipped = jnp.minimum(view, views - 1)
    shift = offsets[t, s]
    count = jnp.float32(0.0)
    for d in range(slots):
        count = count + jnp.where(cover[t, d] < views, 1.0, 0.0)
    scale = jnp.where(view < views, 1.0, 0.0) / jnp.full((8, nz), count, jnp.float32)
    bx = [psf[clipped, 0, k] for k in range(taps)]

    def band(size, axis, offset, high, low, transposed):
        r = lax.broadcasted_iota(jnp.int32, (size, size), 1 if transposed else 0)
        c = lax.broadcasted_iota(jnp.int32, (size, size), 0 if transposed else 1)
        where = c - r - offset + rad
        weight = jnp.zeros((size, size), jnp.float32)
        for k in range(taps):
            weight = jnp.where(where == k, psf[clipped, axis, k], weight)
        h, l = split(weight)
        high[...] = h
        low[...] = l

    def forward(b, d):
        base = source(d) * share

        @pl.loop(0, share // 8)
        def _(i):
            at = pl.ds(pl.multiple_of(base + i * 8, 8), 8)
            x = [cells[b, j, at, :] for j in range(rows + 4 * rad)]
            sums = []
            for r in range(wide):
                total = bx[0] * x[r]
                for k in range(1, taps):
                    total = total + bx[k] * x[r + k]
                sums.append(total)
            data = split(jnp.concatenate(sums, axis=0))
            z = dot3(data, (wzt[0], wzt[1]))
            mid[:, at, :] = z.reshape(wide, 8, nz)

    def middle():
        @pl.loop(0, wide // 2)
        def _(i):
            quotients = []
            for r in (2 * i, 2 * i + 1):
                row = t * rows - rad + r
                inside = jnp.logical_and(row >= 0, row < tiles * rows)
                blurred = dot3((wy[0], wy[1]), split(mid[r]))
                quotients.append(jnp.where(inside, obs[r], 0.0) / blurred)
            for r, quotient in zip((2 * i, 2 * i + 1), quotients):
                mid[r] = dot3((wyt[0], wyt[1]), split(quotient))

    def backward(d, put):
        base = goal(d) * share

        @pl.loop(0, share // 8)
        def _(i):
            at = pl.ds(pl.multiple_of(base + i * 8, 8), 8)
            q = [mid[j, at, :] for j in range(wide)]
            sums = []
            for r in range(rows):
                total = bx[0] * q[r + 2 * rad]
                for k in range(1, taps):
                    total = total + bx[k] * q[r + 2 * rad - k]
                sums.append(total)
            data = split(jnp.concatenate(sums, axis=0))
            z = dot3(data, (wz[0], wz[1])).reshape(rows, 8, nz) * scale[None]
            put(pl.ds(pl.multiple_of(i * 8, 8), 8), z)

    def relayed(b, j, arriving=False):
        whose = ((1, 2, 1, 2, 3, 3) if arriving else (0, 0, 0, 0, 1, 2))[j]
        low = j in (0, 3, 4)
        at = cells.at[b, pl.ds(2 * rad + (0 if low else half), half), cols(whose), :]
        from_input = b == 0 and not arriving and whose == 0
        return pltpu.make_async_remote_copy(
            src_ref=est.at[pl.ds(0 if low else half, half)] if from_input else at,
            dst_ref=at,
            send_sem=gs.at[b, j], recv_sem=gr.at[b, j],
            device_id=peer(1 if j in (0, 2, 5) else 2), device_id_type=pl.DeviceIdType.MESH,
        )

    def summed(b, j):
        source, target, low = ((2, 2, 1), (2, 2, 0), (0, 0, 1), (1, 1, 0), (1, 1, 1), (0, 0, 0))[j]
        part = pl.ds(0 if low else half, half)
        return pltpu.make_async_remote_copy(
            src_ref=sent.at[b, source, part], dst_ref=got.at[b, target, part],
            send_sem=rs.at[b, j], recv_sem=rr.at[b, j],
            device_id=peer(1 if j in (0, 2, 5) else 2), device_id_type=pl.DeviceIdType.MESH,
        )

    def combine(b, source, first):
        @pl.loop(first, first + half)
        def _(r):
            sent[b, source, r] = sent[b, source, r] + got[b, 2, r]

    def update(b, first, count, parts):
        @pl.loop(first, first + count)
        def _(r):
            total = own[r]
            for d in range(parts):
                total = total + got[b, d, r]
            new = cells[b, 2 * rad + r, cols(0), :] * total
            if b == ITERS - 1:
                out[r] = new
            else:
                cells[b + 1, 2 * rad + r, cols(0), :] = new

    def keep(at, z):
        own[:, at, :] = z

    def fill(b):
        @pl.when(jnp.logical_not(has_prev))
        def _():
            cells[b, pl.ds(0, 2 * rad), :, :] = jnp.zeros((2 * rad, ny, nz), jnp.float32)

        @pl.when(jnp.logical_not(has_next))
        def _():
            cells[b, pl.ds(rows + 2 * rad, 2 * rad), :, :] = jnp.zeros((2 * rad, ny, nz), jnp.float32)

    def prepare():
        cells[0, pl.ds(2 * rad, rows), cols(0), :] = est[...]

    def bands():
        band(nz, 2, shift, wzt.at[0], wzt.at[1], True)
        band(nz, 2, shift, wz.at[0], wz.at[1], False)
        band(ny, 1, 0, wy.at[0], wy.at[1], False)
        band(ny, 1, 0, wyt.at[0], wyt.at[1], True)

    def send_back(b, d):
        def put(at, z):
            sent[b, d - 1, :, at, :] = z

        backward(d, put)

    for b in range(ITERS):
        if grid:
            if b == 0:
                for j in range(4):
                    relayed(b, j).start()
                prepare()
            halo_start(b, 0)
            fill(b)
            if b == 0:
                bands()
            for j in range(2):
                relayed(b, j, True).wait_recv()
                relayed(b, 4 + j).start()
            for j in range(2, 4):
                relayed(b, j, True).wait_recv()
                halo_start(b, j - 1)
            halo_wait(b, 0)
            forward(b, 0)
            relayed(b, 4, True).wait_recv()
            relayed(b, 5, True).wait_recv()
            halo_start(b, 3)
            for d in range(1, 4):
                halo_wait(b, d)
                forward(b, d)
        else:
            for d in range(1, slots):
                gather(b, d).start()
            if b == 0:
                prepare()
            halo_start(b, 0)
            fill(b)
            if b == 0:
                bands()
            for d in range(1, slots + 1):
                if d < slots:
                    gather_in(b, d).wait_recv()
                    halo_start(b, d)
                halo_wait(b, d - 1)
                forward(b, d - 1)
        if b == 0:
            obs_copy.wait()
        middle()
        if grid:
            send_back(b, 3)
            summed(b, 0).start()
            summed(b, 1).start()
            send_back(b, 1)
            summed(b, 2).start()
            send_back(b, 2)
            summed(b, 3).start()
            summed(b, 0).wait_recv()
            combine(b, 1, 0)
            summed(b, 4).start()
            summed(b, 1).wait_recv()
            combine(b, 0, half)
            summed(b, 5).start()
            backward(0, keep)
            for first, waits, starts in ((0, (2, 4), (0, 3)), (half, (3, 5), (1, 2))):
                for j in waits:
                    summed(b, j).wait_recv()
                update(b, first, half, 2)
                if b < ITERS - 1:
                    for j in starts:
                        relayed(b + 1, j).start()
        else:
            for d in range(1, slots):
                send_back(b, d)
                scatter(b, d).start()
            backward(0, keep)
            for d in range(1, slots):
                scatter(b, d).wait_recv()
            update(b, 0, rows, slots - 1)

    for b in range(ITERS):
        for d in range(slots):
            halo_sent(b, d)
        if grid:
            for j in range(6):
                relayed(b, j).wait_send()
                summed(b, j).wait_send()
        else:
            for d in range(1, slots):
                gather(b, d).wait_send()
                scatter(b, d).wait_send()


def per_device(tiles, slots, estimate, observed, psf, cover, offsets):
    rows, share, nz = estimate.shape
    wide, ny = observed.shape[2:4]
    f32, bf16, dma = jnp.float32, jnp.bfloat16, pltpu.SemaphoreType.DMA
    vmem = pl.BlockSpec(memory_space=pltpu.VMEM)
    smem = pl.BlockSpec(memory_space=pltpu.SMEM)
    return pl.pallas_call(
        functools.partial(kernel, tiles, slots),
        out_shape=jax.ShapeDtypeStruct(estimate.shape, f32),
        in_specs=[vmem, pl.BlockSpec(memory_space=pl.ANY), smem, smem, smem],
        out_specs=vmem,
        scratch_shapes=[
            pltpu.VMEM((ITERS, 2 * wide - rows, ny, nz), f32),
            pltpu.VMEM((wide, ny, nz), f32),
            pltpu.VMEM((wide, ny, nz), f32),
            pltpu.VMEM((ITERS, slots - 1, rows, share, nz), f32),
            pltpu.VMEM((ITERS, slots - 1, rows, share, nz), f32),
            pltpu.VMEM((rows, share, nz), f32),
            pltpu.VMEM((2, nz, nz), bf16),
            pltpu.VMEM((2, nz, nz), bf16),
            pltpu.VMEM((2, ny, ny), bf16),
            pltpu.VMEM((2, ny, ny), bf16),
            dma,
            dma((ITERS, slots + 2)), dma((ITERS, slots + 2)),
            dma((ITERS, slots, 2)), dma((ITERS, slots, 2)),
            dma((ITERS, slots + 2)), dma((ITERS, slots + 2)),
        ],
        compiler_params=pltpu.CompilerParams(
            collective_id=0, has_side_effects=True, vmem_limit_bytes=48 * 1024 * 1024
        ),
    )(estimate, observed, psf, cover, offsets)


def solution(mesh):
    placed = (P("tile", "view", None), P("view", "tile", None, None, None), P(), P(), P())
    return jax.shard_map(
        functools.partial(per_device, mesh.shape["tile"], mesh.shape["view"]),
        mesh=mesh, in_specs=placed, out_specs=P("tile", "view", None), check_vma=False,
    )
```

```python
import functools

import jax
import jax.numpy as jnp
from jax import lax
from jax.experimental import pallas as pl
from jax.experimental.pallas import tpu as pltpu
from jax.sharding import PartitionSpec as P

ITERS = 2


def split(x):
    high = x.astype(jnp.bfloat16)
    low = (x - high.astype(jnp.float32)).astype(jnp.bfloat16)
    return high, low


def dot(a, b):
    return jnp.dot(a, b, preferred_element_type=jnp.float32)


def dot3(a, b):
    (ah, al), (bh, bl) = a, b
    return dot(ah, bh) + (dot(ah, bl) + dot(al, bh))


def kernel(
    tiles, slots, est, obs_hbm, psf, cover, offsets, out,
    cells, mid, obs, sent, got, own, wz, wzt, wy, wyt,
    obs_sem, est_sem, gs, gr, hs, hr, rs, rr,
):
    t = lax.axis_index("tile")
    s = lax.axis_index("view")
    rows, share, nz = est.shape
    ny = mid.shape[1]
    taps, _, views = psf.shape
    rad = taps // 2
    wide = rows + 2 * rad
    has_prev, has_next = t > 0, t < tiles - 1

    half, chunk = share // 2, rows // 2
    grid = slots == 4 and share % 16 == 0
    around = (s, s + 1 - 2 * lax.rem(s, 2), lax.rem(s + 2, 4), 3 - s)

    def source(d):
        return around[d] if grid else lax.rem(s + slots - d, slots)

    def goal(d):
        return around[d] if grid else lax.rem(s + d, slots)

    def cols(d):
        return pl.ds(pl.multiple_of(source(d) * share, 8), share)

    def peer(d):
        return {"view": goal(d)}

    obs_copy = pltpu.make_async_copy(obs_hbm.at[0, 0], obs, obs_sem)
    est_copy = pltpu.make_async_copy(est, cells.at[0, pl.ds(2 * rad, rows), cols(0), :], est_sem)
    est_copy.start()
    obs_copy.start()

    barrier = pltpu.get_barrier_semaphore()
    for d in range(1, slots):
        pl.semaphore_signal(barrier, inc=1, device_id=peer(d), device_id_type=pl.DeviceIdType.MESH)

    @pl.when(has_prev)
    def _():
        pl.semaphore_signal(barrier, inc=1, device_id={"tile": t - 1}, device_id_type=pl.DeviceIdType.MESH)

    @pl.when(has_next)
    def _():
        pl.semaphore_signal(barrier, inc=1, device_id={"tile": t + 1}, device_id_type=pl.DeviceIdType.MESH)

    neighbours = has_prev.astype(jnp.int32) + has_next.astype(jnp.int32)
    pl.semaphore_wait(barrier, slots - 1 + neighbours)

    def gather(b, d):
        src = est if b == 0 else cells.at[b, pl.ds(2 * rad, rows), cols(0), :]
        return pltpu.make_async_remote_copy(
            src_ref=src,
            dst_ref=cells.at[b, pl.ds(2 * rad, rows), cols(0), :],
            send_sem=gs.at[b, 0, d], recv_sem=gr.at[b, 0, d],
            device_id=peer(d), device_id_type=pl.DeviceIdType.MESH,
        )

    def gather_in(b, d):
        block = cells.at[b, pl.ds(2 * rad, rows), cols(d), :]
        return pltpu.make_async_remote_copy(
            src_ref=block, dst_ref=block,
            send_sem=gs.at[b, 0, d], recv_sem=gr.at[b, 0, d],
            device_id=peer(d), device_id_type=pl.DeviceIdType.MESH,
        )

    def halo(b, d, up):
        first, to = (rows, 0) if up else (2 * rad, rows + 2 * rad)
        return pltpu.make_async_remote_copy(
            src_ref=cells.at[b, pl.ds(first, 2 * rad), cols(d), :],
            dst_ref=cells.at[b, pl.ds(to, 2 * rad), cols(d), :],
            send_sem=hs.at[b, d, int(up)], recv_sem=hr.at[b, d, int(up)],
            device_id={"tile": t + 1 if up else t - 1}, device_id_type=pl.DeviceIdType.MESH,
        )

    def halo_start(b, d):
        @pl.when(has_next)
        def _():
            halo(b, d, True).start()

        @pl.when(has_prev)
        def _():
            halo(b, d, False).start()

    def halo_wait(b, d):
        @pl.when(has_prev)
        def _():
            halo(b, d, True).wait_recv()

        @pl.when(has_next)
        def _():
            halo(b, d, False).wait_recv()

    def halo_sent(b, d):
        @pl.when(has_next)
        def _():
            halo(b, d, True).wait_send()

        @pl.when(has_prev)
        def _():
            halo(b, d, False).wait_send()

    def scatter(b, d):
        return pltpu.make_async_remote_copy(
            src_ref=sent.at[b, d - 1], dst_ref=got.at[b, d - 1],
            send_sem=rs.at[b, 0, d], recv_sem=rr.at[b, 0, d],
            device_id=peer(d), device_id_type=pl.DeviceIdType.MESH,
        )

    view = cover[s, t]
    clipped = jnp.minimum(view, views - 1)
    shift = offsets[s, t]
    count = jnp.float32(0.0)
    for d in range(slots):
        count = count + jnp.where(cover[d, t] < views, 1.0, 0.0)
    scale = jnp.where(view < views, 1.0, 0.0) / jnp.full((8, nz), count, jnp.float32)
    bx = [psf[k, 0, clipped] for k in range(taps)]

    def band(size, axis, offset, high, low, transposed):
        r = lax.broadcasted_iota(jnp.int32, (size, size), 1 if transposed else 0)
        c = lax.broadcasted_iota(jnp.int32, (size, size), 0 if transposed else 1)
        where = c - r - offset + rad
        weight = jnp.zeros((size, size), jnp.float32)
        for k in range(taps):
            weight = jnp.where(where == k, psf[k, axis, clipped], weight)
        h, l = split(weight)
        high[...] = h
        low[...] = l

    def forward(b, d):
        base = source(d) * share

        @pl.loop(0, share // 8)
        def _(i):
            at = pl.ds(pl.multiple_of(base + i * 8, 8), 8)
            x = [cells[b, j, at, :] for j in range(rows + 4 * rad)]
            sums = []
            for r in range(wide):
                total = bx[0] * x[r]
                for k in range(1, taps):
                    total = total + bx[k] * x[r + k]
                sums.append(total)
            data = split(jnp.concatenate(sums, axis=0))
            z = dot3(data, (wzt[0], wzt[1]))
            mid[:, at, :] = z.reshape(wide, 8, nz)

    def middle(begin, end):
        @pl.loop(begin, end)
        def _(i):
            quotients = []
            for r in (2 * i, 2 * i + 1):
                row = t * rows - rad + r
                inside = jnp.logical_and(row >= 0, row < tiles * rows)
                blurred = dot3((wy[0], wy[1]), split(mid[r]))
                quotients.append(jnp.where(inside, obs[r], 0.0) / blurred)
            for r, quotient in zip((2 * i, 2 * i + 1), quotients):
                mid[r] = dot3((wyt[0], wyt[1]), split(quotient))

    step = 16 if grid else 8

    def backward(d, put, first, number):
        base = goal(d) * share

        @pl.loop(0, share // step)
        def _(i):
            at = pl.ds(pl.multiple_of(base + i * step, 8), step)
            q = [mid[first + j, at, :] for j in range(number + 2 * rad)]
            sums = []
            for r in range(number):
                total = bx[0] * q[r + 2 * rad]
                for k in range(1, taps):
                    total = total + bx[k] * q[r + 2 * rad - k]
                sums.append(total)
            data = split(jnp.concatenate(sums, axis=0))
            z = dot3(data, (wz[0], wz[1])) * scale[0:1]
            put(pl.ds(first, number), pl.ds(pl.multiple_of(i * step, 8), step), z.reshape(number, step, nz))

    def relayed(b, c, j, arriving=False):
        whose = ((1, 2, 1, 2, 3, 3) if arriving else (0, 0, 0, 0, 1, 2))[j]
        side = 0 if j in (0, 3, 4) else half
        columns = pl.ds(pl.multiple_of(source(whose) * share + side, 8), half)
        at = cells.at[b, pl.ds(2 * rad + c * chunk, chunk), columns, :]
        from_input = b == 0 and not arriving and whose == 0
        return pltpu.make_async_remote_copy(
            src_ref=est.at[pl.ds(c * chunk, chunk), pl.ds(side, half), :] if from_input else at,
            dst_ref=at,
            send_sem=gs.at[b, c, j], recv_sem=gr.at[b, c, j],
            device_id=peer(1 if j in (0, 2, 5) else 2), device_id_type=pl.DeviceIdType.MESH,
        )

    def summed(b, c, j):
        origin, target, side = ((2, 2, 0), (2, 2, half), (0, 0, 0), (1, 1, half), (1, 1, 0), (0, 0, half))[j]
        part = (pl.ds(c * chunk, chunk), pl.ds(side, half))
        return pltpu.make_async_remote_copy(
            src_ref=sent.at[b, origin, *part], dst_ref=got.at[b, target, *part],
            send_sem=rs.at[b, c, j], recv_sem=rr.at[b, c, j],
            device_id=peer(1 if j in (0, 2, 5) else 2), device_id_type=pl.DeviceIdType.MESH,
        )

    def combine(b, c):
        for j, origin, side in ((0, 1, 0), (1, 0, half)):
            summed(b, c, j).wait_recv()
            part = (pl.ds(c * chunk, chunk), pl.ds(side, half))
            sent[b, origin, *part] = sent[b, origin, *part] + got[b, 2, *part]
            summed(b, c, 4 + j).start()

    def update(b, first, count, parts):
        @pl.loop(first, first + count)
        def _(r):
            total = own[r]
            for d in range(parts):
                total = total + got[b, d, r]
            new = cells[b, 2 * rad + r, cols(0), :] * total
            if b == ITERS - 1:
                out[r] = new
            else:
                cells[b + 1, 2 * rad + r, cols(0), :] = new

    def keep(part, at, z):
        own[part, at, :] = z

    def fill(b):
        @pl.when(jnp.logical_not(has_prev))
        def _():
            cells[b, pl.ds(0, 2 * rad), :, :] = jnp.zeros((2 * rad, ny, nz), jnp.float32)

        @pl.when(jnp.logical_not(has_next))
        def _():
            cells[b, pl.ds(rows + 2 * rad, 2 * rad), :, :] = jnp.zeros((2 * rad, ny, nz), jnp.float32)

    def prepare():
        est_copy.wait()

    def bands():
        band(nz, 2, shift, wzt.at[0], wzt.at[1], True)
        band(nz, 2, shift, wz.at[0], wz.at[1], False)
        band(ny, 1, 0, wy.at[0], wy.at[1], False)
        band(ny, 1, 0, wyt.at[0], wyt.at[1], True)

    def send_back(b, d, first, number):
        def put(part, at, z):
            sent[b, d - 1, part, at, :] = z

        backward(d, put, first, number)

    for b in range(ITERS):
        if grid:
            if b == 0:
                for c in range(2):
                    for j in range(4):
                        relayed(b, c, j).start()
                prepare()
            halo_start(b, 0)
            fill(b)
            if b == 0:
                bands()
            for c in range(2):
                for j in range(2):
                    relayed(b, c, j, True).wait_recv()
                    relayed(b, c, 4 + j).start()
            for j in range(2, 4):
                for c in range(2):
                    relayed(b, c, j, True).wait_recv()
                halo_start(b, j - 1)
            halo_wait(b, 0)
            forward(b, 0)
            for c in range(2):
                relayed(b, c, 4, True).wait_recv()
                relayed(b, c, 5, True).wait_recv()
            halo_start(b, 3)
            for d in range(1, 4):
                halo_wait(b, d)
                forward(b, d)
        else:
            for d in range(1, slots):
                gather(b, d).start()
            if b == 0:
                prepare()
            halo_start(b, 0)
            fill(b)
            if b == 0:
                bands()
            for d in range(1, slots + 1):
                if d < slots:
                    gather_in(b, d).wait_recv()
                    halo_start(b, d)
                halo_wait(b, d - 1)
                forward(b, d - 1)
        if b == 0:
            obs_copy.wait()
        if grid:
            ready = (chunk + 2 * rad + 1) // 2
            for c, begin, end in ((0, 0, ready), (1, ready, wide // 2)):
                middle(begin, end)
                if c == 1:
                    combine(b, 0)
                for d, copies in ((3, (0, 1)), (1, (2,)), (2, (3,))):
                    send_back(b, d, c * chunk, chunk)
                    for j in copies:
                        summed(b, c, j).start()
            backward(0, keep, 0, chunk)
            combine(b, 1)
            backward(0, keep, chunk, chunk)
            for c in range(2):
                for j in range(2, 6):
                    summed(b, c, j).wait_recv()
                update(b, c * chunk, chunk, 2)
                if b < ITERS - 1:
                    for j in range(4):
                        relayed(b + 1, c, j).start()
        else:
            middle(0, wide // 2)
            for d in range(1, slots):
                send_back(b, d, 0, rows)
                scatter(b, d).start()
            backward(0, keep, 0, rows)
            for d in range(1, slots):
                scatter(b, d).wait_recv()
            update(b, 0, rows, slots - 1)

    for b in range(ITERS):
        for d in range(slots):
            halo_sent(b, d)
        if grid:
            for c in range(2):
                for j in range(6):
                    relayed(b, c, j).wait_send()
                    summed(b, c, j).wait_send()
        else:
            for d in range(1, slots):
                gather(b, d).wait_send()
                scatter(b, d).wait_send()


def per_device(tiles, slots, estimate, observed, psf, cover, offsets):
    rows, share, nz = estimate.shape
    wide, ny = observed.shape[2:4]
    f32, bf16, dma = jnp.float32, jnp.bfloat16, pltpu.SemaphoreType.DMA
    vmem = pl.BlockSpec(memory_space=pltpu.VMEM)
    smem = pl.BlockSpec(memory_space=pltpu.SMEM)
    return pl.pallas_call(
        functools.partial(kernel, tiles, slots),
        out_shape=jax.ShapeDtypeStruct(estimate.shape, f32),
        in_specs=[pl.BlockSpec(memory_space=pl.ANY)] * 2 + [smem] * 3,
        out_specs=vmem,
        scratch_shapes=[
            pltpu.VMEM((ITERS, 2 * wide - rows, ny, nz), f32),
            pltpu.VMEM((wide, ny, nz), f32),
            pltpu.VMEM((wide, ny, nz), f32),
            pltpu.VMEM((ITERS, slots - 1, rows, share, nz), f32),
            pltpu.VMEM((ITERS, slots - 1, rows, share, nz), f32),
            pltpu.VMEM((rows, share, nz), f32),
            pltpu.VMEM((2, nz, nz), bf16),
            pltpu.VMEM((2, nz, nz), bf16),
            pltpu.VMEM((2, ny, ny), bf16),
            pltpu.VMEM((2, ny, ny), bf16),
            dma, dma,
            dma((ITERS, 2, slots + 2)), dma((ITERS, 2, slots + 2)),
            dma((ITERS, slots, 2)), dma((ITERS, slots, 2)),
            dma((ITERS, 2, slots + 2)), dma((ITERS, 2, slots + 2)),
        ],
        compiler_params=pltpu.CompilerParams(
            collective_id=0, has_side_effects=True, vmem_limit_bytes=60 * 1024 * 1024
        ),
    )(estimate, observed, psf.transpose(2, 1, 0), cover.T, offsets.T)


def solution(mesh):
    placed = (P("tile", "view", None), P("view", "tile", None, None, None), P(), P(), P())
    return jax.shard_map(
        functools.partial(per_device, mesh.shape["tile"], mesh.shape["view"]),
        mesh=mesh, in_specs=placed, out_specs=P("tile", "view", None), check_vma=False,
    )
```

```python
import functools

import jax
import jax.numpy as jnp
from jax import lax
from jax.experimental import pallas as pl
from jax.experimental.pallas import tpu as pltpu
from jax.sharding import PartitionSpec as P

ITERS = 2


def split(x):
    high = x.astype(jnp.bfloat16)
    low = (x - high.astype(jnp.float32)).astype(jnp.bfloat16)
    return high, low


def dot(a, b):
    return jnp.dot(a, b, preferred_element_type=jnp.float32)


def dot3(a, b):
    (ah, al), (bh, bl) = a, b
    return dot(ah, bh) + (dot(ah, bl) + dot(al, bh))


def kernel(
    tiles, slots, est, obs_hbm, psf, cover, offsets, out,
    cells, mid, obs, sent, got, own, wz, wzt, wy, wyt,
    obs_sem, est_sem, gs, gr, hs, hr, rs, rr,
):
    t = lax.axis_index("tile")
    s = lax.axis_index("view")
    rows, share, nz = est.shape
    ny = mid.shape[1]
    taps, _, views = psf.shape
    rad = taps // 2
    wide = rows + 2 * rad
    has_prev, has_next = t > 0, t < tiles - 1

    half, chunk = share // 2, rows // 2
    grid = slots == 4 and share % 16 == 0
    around = (s, s + 1 - 2 * lax.rem(s, 2), lax.rem(s + 2, 4), 3 - s)

    def source(d):
        return around[d] if grid else lax.rem(s + slots - d, slots)

    def goal(d):
        return around[d] if grid else lax.rem(s + d, slots)

    def cols(d):
        return pl.ds(pl.multiple_of(source(d) * share, 8), share)

    def peer(d):
        return {"view": goal(d)}

    obs_copy = pltpu.make_async_copy(obs_hbm.at[0, 0], obs, obs_sem)
    est_copy = pltpu.make_async_copy(est, cells.at[0, pl.ds(2 * rad, rows), cols(0), :], est_sem)
    est_copy.start()
    obs_copy.start()

    barrier = pltpu.get_barrier_semaphore()
    for d in range(1, slots):
        pl.semaphore_signal(barrier, inc=1, device_id=peer(d), device_id_type=pl.DeviceIdType.MESH)

    @pl.when(has_prev)
    def _():
        pl.semaphore_signal(barrier, inc=1, device_id={"tile": t - 1}, device_id_type=pl.DeviceIdType.MESH)

    @pl.when(has_next)
    def _():
        pl.semaphore_signal(barrier, inc=1, device_id={"tile": t + 1}, device_id_type=pl.DeviceIdType.MESH)

    neighbours = has_prev.astype(jnp.int32) + has_next.astype(jnp.int32)
    pl.semaphore_wait(barrier, slots - 1 + neighbours)

    def gather(b, d):
        src = est if b == 0 else cells.at[b, pl.ds(2 * rad, rows), cols(0), :]
        return pltpu.make_async_remote_copy(
            src_ref=src,
            dst_ref=cells.at[b, pl.ds(2 * rad, rows), cols(0), :],
            send_sem=gs.at[b, 0, d], recv_sem=gr.at[b, 0, d],
            device_id=peer(d), device_id_type=pl.DeviceIdType.MESH,
        )

    def gather_in(b, d):
        block = cells.at[b, pl.ds(2 * rad, rows), cols(d), :]
        return pltpu.make_async_remote_copy(
            src_ref=block, dst_ref=block,
            send_sem=gs.at[b, 0, d], recv_sem=gr.at[b, 0, d],
            device_id=peer(d), device_id_type=pl.DeviceIdType.MESH,
        )

    def halo(b, d, up):
        first, to = (rows, 0) if up else (2 * rad, rows + 2 * rad)
        return pltpu.make_async_remote_copy(
            src_ref=cells.at[b, pl.ds(first, 2 * rad), cols(d), :],
            dst_ref=cells.at[b, pl.ds(to, 2 * rad), cols(d), :],
            send_sem=hs.at[b, d, int(up)], recv_sem=hr.at[b, d, int(up)],
            device_id={"tile": t + 1 if up else t - 1}, device_id_type=pl.DeviceIdType.MESH,
        )

    def halo_start(b, d):
        @pl.when(has_next)
        def _():
            halo(b, d, True).start()

        @pl.when(has_prev)
        def _():
            halo(b, d, False).start()

    def halo_wait(b, d):
        @pl.when(has_prev)
        def _():
            halo(b, d, True).wait_recv()

        @pl.when(has_next)
        def _():
            halo(b, d, False).wait_recv()

    def halo_sent(b, d):
        @pl.when(has_next)
        def _():
            halo(b, d, True).wait_send()

        @pl.when(has_prev)
        def _():
            halo(b, d, False).wait_send()

    def scatter(b, d):
        return pltpu.make_async_remote_copy(
            src_ref=sent.at[b, d - 1], dst_ref=got.at[b, d - 1],
            send_sem=rs.at[b, 0, d], recv_sem=rr.at[b, 0, d],
            device_id=peer(d), device_id_type=pl.DeviceIdType.MESH,
        )

    view = cover[s, t]
    clipped = jnp.minimum(view, views - 1)
    shift = offsets[s, t]
    count = jnp.float32(0.0)
    for d in range(slots):
        count = count + jnp.where(cover[d, t] < views, 1.0, 0.0)
    scale = jnp.where(view < views, 1.0, 0.0) / jnp.full((8, nz), count, jnp.float32)
    bx = [psf[k, 0, clipped] for k in range(taps)]

    def band(size, axis, offset, high, low, transposed):
        r = lax.broadcasted_iota(jnp.int32, (size, size), 1 if transposed else 0)
        c = lax.broadcasted_iota(jnp.int32, (size, size), 0 if transposed else 1)
        where = c - r - offset + rad
        weight = jnp.zeros((size, size), jnp.float32)
        for k in range(taps):
            weight = jnp.where(where == k, psf[k, axis, clipped], weight)
        h, l = split(weight)
        high[...] = h
        low[...] = l

    def forward(b, d):
        base = source(d) * share

        @pl.loop(0, share // step)
        def _(i):
            at = pl.ds(pl.multiple_of(base + i * step, 8), step)
            x = [cells[b, j, at, :] for j in range(rows + 4 * rad)]
            sums = []
            for r in range(wide):
                total = bx[0] * x[r]
                for k in range(1, taps):
                    total = total + bx[k] * x[r + k]
                sums.append(total)
            data = split(jnp.concatenate(sums, axis=0))
            z = dot3(data, (wzt[0], wzt[1]))
            mid[:, at, :] = z.reshape(wide, step, nz)

    def middle(begin, end):
        @pl.loop(begin, end)
        def _(i):
            quotients = []
            for r in (2 * i, 2 * i + 1):
                row = t * rows - rad + r
                inside = jnp.logical_and(row >= 0, row < tiles * rows)
                blurred = dot3((wy[0], wy[1]), split(mid[r]))
                quotients.append(jnp.where(inside, obs[r], 0.0) / blurred)
            for r, quotient in zip((2 * i, 2 * i + 1), quotients):
                mid[r] = dot3((wyt[0], wyt[1]), split(quotient))

    step = 16 if grid else 8

    def backward(d, put, first, number):
        base = goal(d) * share

        @pl.loop(0, share // step)
        def _(i):
            at = pl.ds(pl.multiple_of(base + i * step, 8), step)
            q = [mid[first + j, at, :] for j in range(number + 2 * rad)]
            sums = []
            for r in range(number):
                total = bx[0] * q[r + 2 * rad]
                for k in range(1, taps):
                    total = total + bx[k] * q[r + 2 * rad - k]
                sums.append(total)
            data = split(jnp.concatenate(sums, axis=0))
            z = dot3(data, (wz[0], wz[1])) * scale[0:1]
            put(pl.ds(first, number), pl.ds(pl.multiple_of(i * step, 8), step), z.reshape(number, step, nz))

    def relayed(b, c, j, arriving=False):
        whose = ((1, 2, 1, 2, 3, 3) if arriving else (0, 0, 0, 0, 1, 2))[j]
        side = 0 if j in (0, 3, 4) else half
        columns = pl.ds(pl.multiple_of(source(whose) * share + side, 8), half)
        at = cells.at[b, pl.ds(2 * rad + c * chunk, chunk), columns, :]
        from_input = b == 0 and not arriving and whose == 0
        return pltpu.make_async_remote_copy(
            src_ref=est.at[pl.ds(c * chunk, chunk), pl.ds(side, half), :] if from_input else at,
            dst_ref=at,
            send_sem=gs.at[b, c, j], recv_sem=gr.at[b, c, j],
            device_id=peer(1 if j in (0, 2, 5) else 2), device_id_type=pl.DeviceIdType.MESH,
        )

    def summed(b, c, j):
        origin, target, side = ((2, 2, 0), (2, 2, half), (0, 0, 0), (1, 1, half), (1, 1, 0), (0, 0, half))[j]
        part = (pl.ds(c * chunk, chunk), pl.ds(side, half))
        return pltpu.make_async_remote_copy(
            src_ref=sent.at[b, origin, *part], dst_ref=got.at[b, target, *part],
            send_sem=rs.at[b, c, j], recv_sem=rr.at[b, c, j],
            device_id=peer(1 if j in (0, 2, 5) else 2), device_id_type=pl.DeviceIdType.MESH,
        )

    def combine(b, c):
        for j, origin, side in ((0, 1, 0), (1, 0, half)):
            summed(b, c, j).wait_recv()
            part = (pl.ds(c * chunk, chunk), pl.ds(side, half))
            sent[b, origin, *part] = sent[b, origin, *part] + got[b, 2, *part]
            summed(b, c, 4 + j).start()

    def update(b, first, count, parts):
        @pl.loop(first, first + count)
        def _(r):
            total = own[r]
            for d in range(parts):
                total = total + got[b, d, r]
            new = cells[b, 2 * rad + r, cols(0), :] * total
            if b == ITERS - 1:
                out[r] = new
            else:
                cells[b + 1, 2 * rad + r, cols(0), :] = new

    def keep(part, at, z):
        own[part, at, :] = z

    def fill(b):
        @pl.when(jnp.logical_not(has_prev))
        def _():
            cells[b, pl.ds(0, 2 * rad), :, :] = jnp.zeros((2 * rad, ny, nz), jnp.float32)

        @pl.when(jnp.logical_not(has_next))
        def _():
            cells[b, pl.ds(rows + 2 * rad, 2 * rad), :, :] = jnp.zeros((2 * rad, ny, nz), jnp.float32)

    def prepare():
        est_copy.wait()

    def bands():
        band(nz, 2, shift, wzt.at[0], wzt.at[1], True)
        band(nz, 2, shift, wz.at[0], wz.at[1], False)
        band(ny, 1, 0, wy.at[0], wy.at[1], False)
        band(ny, 1, 0, wyt.at[0], wyt.at[1], True)

    def send_back(b, d, first, number):
        def put(part, at, z):
            sent[b, d - 1, part, at, :] = z

        backward(d, put, first, number)

    for b in range(ITERS):
        if grid:
            if b == 0:
                for c in range(2):
                    for j in range(4):
                        relayed(b, c, j).start()
                prepare()
            halo_start(b, 0)
            fill(b)
            if b == 0:
                bands()
            for c in range(2):
                for j in range(2):
                    relayed(b, c, j, True).wait_recv()
                    relayed(b, c, 4 + j).start()
            for j in range(2, 4):
                for c in range(2):
                    relayed(b, c, j, True).wait_recv()
                halo_start(b, j - 1)
            halo_wait(b, 0)
            forward(b, 0)
            for c in range(2):
                relayed(b, c, 4, True).wait_recv()
                relayed(b, c, 5, True).wait_recv()
            halo_start(b, 3)
            for d in range(1, 4):
                halo_wait(b, d)
                forward(b, d)
        else:
            for d in range(1, slots):
                gather(b, d).start()
            if b == 0:
                prepare()
            halo_start(b, 0)
            fill(b)
            if b == 0:
                bands()
            for d in range(1, slots + 1):
                if d < slots:
                    gather_in(b, d).wait_recv()
                    halo_start(b, d)
                halo_wait(b, d - 1)
                forward(b, d - 1)
        if b == 0:
            obs_copy.wait()
        if grid:
            ready = (chunk + 2 * rad + 1) // 2
            for c, begin, end in ((0, 0, ready), (1, ready, wide // 2)):
                middle(begin, end)
                if c == 1:
                    combine(b, 0)
                for d, copies in ((3, (0, 1)), (1, (2,)), (2, (3,))):
                    send_back(b, d, c * chunk, chunk)
                    for j in copies:
                        summed(b, c, j).start()
            backward(0, keep, 0, chunk)
            combine(b, 1)
            backward(0, keep, chunk, chunk)
            for c in range(2):
                for j in range(2, 6):
                    summed(b, c, j).wait_recv()
                update(b, c * chunk, chunk, 2)
                if b < ITERS - 1:
                    for j in range(4):
                        relayed(b + 1, c, j).start()
        else:
            middle(0, wide // 2)
            for d in range(1, slots):
                send_back(b, d, 0, rows)
                scatter(b, d).start()
            backward(0, keep, 0, rows)
            for d in range(1, slots):
                scatter(b, d).wait_recv()
            update(b, 0, rows, slots - 1)

    for b in range(ITERS):
        for d in range(slots):
            halo_sent(b, d)
        if grid:
            for c in range(2):
                for j in range(6):
                    relayed(b, c, j).wait_send()
                    summed(b, c, j).wait_send()
        else:
            for d in range(1, slots):
                gather(b, d).wait_send()
                scatter(b, d).wait_send()


def per_device(tiles, slots, estimate, observed, psf, cover, offsets):
    rows, share, nz = estimate.shape
    wide, ny = observed.shape[2:4]
    f32, bf16, dma = jnp.float32, jnp.bfloat16, pltpu.SemaphoreType.DMA
    vmem = pl.BlockSpec(memory_space=pltpu.VMEM)
    smem = pl.BlockSpec(memory_space=pltpu.SMEM)
    return pl.pallas_call(
        functools.partial(kernel, tiles, slots),
        out_shape=jax.ShapeDtypeStruct(estimate.shape, f32),
        in_specs=[pl.BlockSpec(memory_space=pl.ANY)] * 2 + [smem] * 3,
        out_specs=vmem,
        scratch_shapes=[
            pltpu.VMEM((ITERS, 2 * wide - rows, ny, nz), f32),
            pltpu.VMEM((wide, ny, nz), f32),
            pltpu.VMEM((wide, ny, nz), f32),
            pltpu.VMEM((ITERS, slots - 1, rows, share, nz), f32),
            pltpu.VMEM((ITERS, slots - 1, rows, share, nz), f32),
            pltpu.VMEM((rows, share, nz), f32),
            pltpu.VMEM((2, nz, nz), bf16),
            pltpu.VMEM((2, nz, nz), bf16),
            pltpu.VMEM((2, ny, ny), bf16),
            pltpu.VMEM((2, ny, ny), bf16),
            dma, dma,
            dma((ITERS, 2, slots + 2)), dma((ITERS, 2, slots + 2)),
            dma((ITERS, slots, 2)), dma((ITERS, slots, 2)),
            dma((ITERS, 2, slots + 2)), dma((ITERS, 2, slots + 2)),
        ],
        compiler_params=pltpu.CompilerParams(
            collective_id=0, has_side_effects=True, vmem_limit_bytes=60 * 1024 * 1024
        ),
    )(estimate, observed, psf.transpose(2, 1, 0), cover.T, offsets.T)


def solution(mesh):
    placed = (P("tile", "view", None), P("view", "tile", None, None, None), P(), P(), P())
    return jax.shard_map(
        functools.partial(per_device, mesh.shape["tile"], mesh.shape["view"]),
        mesh=mesh, in_specs=placed, out_specs=P("tile", "view", None), check_vma=False,
    )
```
